32 devices in a mesh: groups: 2 (over x), tensor: 16 (over z, y, core).
Axes of the slice: x: 2, y: 2, z: 4, core: 2. Of those that a mesh axis runs over, the one named last changes fastest.
Arguments:
- layer_input: bfloat16 [64, 8192], P(('groups', 'tensor')), parts along dimension 0, may hold values from -6 to 6
- cotangent: bfloat16 [64, 8192], P(('groups', 'tensor')), parts along dimension 0, may hold values from -3 to 3
- gate_values: bfloat16 [64, 14336], P('groups', 'tensor'), parts along dimension 0, may hold values from -6 to 6
- up_values: bfloat16 [64, 14336], P('groups', 'tensor'), parts along dimension 0, may hold values from -6 to 6
- gate_weight: bfloat16 [16384, 14336], P('groups', 'tensor'), parts along dimension 0, may hold values from -0.0625 to 0.0625
- up_weight: bfloat16 [16384, 14336], P('groups', 'tensor'), parts along dimension 0, may hold values from -0.0625 to 0.0625
- down_weight: bfloat16 [28672, 8192], P(('groups', 'tensor')), parts along dimension 0, may hold values from -0.046875 to 0.046875
Outputs:
- input_grad: bfloat16 [64, 8192], P(('groups', 'tensor')), parts along dimension 0
- gate_grad: bfloat16 [16384, 14336], P('groups', 'tensor'), parts along dimension 0
- up_grad: bfloat16 [16384, 14336], P('groups', 'tensor'), parts along dimension 0
- down_grad: bfloat16 [28672, 8192], P(('groups', 'tensor')), parts along dimension 0
- factor: bfloat16 [16384, 8192], P(('groups', 'tensor')), parts along dimension 0
The draws below stay inside these ranges and needn't reach their ends.
There are 2 independent parts, one for each index of `groups`. The reference program is written for one: setup_inputs(seed, part) draws one part's arguments, and reference() takes and returns one part's arrays. A program takes and returns all parts, laid end to end along the dimension named above; each array names one. Nothing has to cross between parts.
All inputs are finite; a program needn't handle non-finite values.
Results may differ from the reference program's by a relative error of at most 0.0049.
Values may be sent and summed in bfloat16 or wider, within the bound.
A program may use at most 192 MiB of HBM per device.

```python
import jax
import jax.numpy as jnp
from jax import lax

D = 8192
FF = 14336
TOKENS = 32


def level_of(rng, shape, pieces, low, high):
    def one(dim, shards_of):
        heights = jax.random.uniform(jax.random.fold_in(jax.random.fold_in(rng, 6), dim), (shards_of,), jnp.float32, low / len(pieces), high / len(pieces))
        return jnp.repeat(jnp.exp(heights), shape[dim] // shards_of).reshape((-1,) + (1,) * (len(shape) - dim - 1))

    level = one(*pieces[0])
    for cut in pieces[1:]:
        level = level * one(*cut)
    return level


def gaussian(key, shape, width, limit, shards=(), held_as=jnp.bfloat16):
    drawn = jax.random.normal(key, shape, jnp.float32) * width
    if len(shards) > 0:
        drawn = level_of(key, shape, shards, -0.22, 0.18) * drawn
    return jnp.clip(drawn, min=-limit, max=limit).astype(held_as)


def setup_inputs(seed: int = 0, part: int = 0) -> dict:
    splits = jax.random.split(jax.random.key(seed), 8)
    part_splits = jax.random.split(jax.random.fold_in(splits[7], part), 8)
    return {
        "layer_input": gaussian(part_splits[0], (TOKENS, D), 1.0, 6.0, ((0, 16),)),
        "cotangent": gaussian(part_splits[1], (TOKENS, D), 0.5, 3.0, ((0, 16),)),
        "gate_values": gaussian(part_splits[2], (TOKENS, FF), 1.0, 6.0, ((1, 16),)),
        "up_values": gaussian(part_splits[3], (TOKENS, FF), 1.0, 6.0, ((1, 16),)),
        "gate_weight": gaussian(part_splits[4], (D, FF), D ** -0.5, 0.0625, ((1, 16),)),
        "up_weight": gaussian(part_splits[5], (D, FF), D ** -0.5, 0.0625, ((1, 16),)),
        "down_weight": gaussian(part_splits[6], (FF, D), FF ** -0.5, 0.046875, ((0, 16),)),
    }


def reference(layer_input, cotangent, gate_values, up_values, gate_weight, up_weight, down_weight):
    gate_float = gate_values.astype(jnp.float32)
    up_float = up_values.astype(jnp.float32)
    sigma = jax.nn.sigmoid(gate_float)
    activated = gate_float * sigma
    hidden = (activated * up_float).astype(jnp.bfloat16)
    hidden_grad = lax.dot_general(cotangent, down_weight, (((1,), (1,)), ((), ())), preferred_element_type=jnp.float32)
    gate_delta = (hidden_grad * up_float * sigma * (1.0 + gate_float * (1.0 - sigma))).astype(jnp.bfloat16)
    up_delta = (hidden_grad * activated).astype(jnp.bfloat16)
    down_grad = lax.dot_general(hidden, cotangent, (((0,), (0,)), ((), ())), preferred_element_type=jnp.float32).astype(jnp.bfloat16)
    gate_grad = lax.dot_general(layer_input, gate_delta, (((0,), (0,)), ((), ())), preferred_element_type=jnp.float32).astype(jnp.bfloat16)
    up_grad = lax.dot_general(layer_input, up_delta, (((0,), (0,)), ((), ())), preferred_element_type=jnp.float32).astype(jnp.bfloat16)
    input_sum = lax.dot_general(gate_delta, gate_weight, (((1,), (1,)), ((), ())), preferred_element_type=jnp.float32)
    input_sum = input_sum + lax.dot_general(up_delta, up_weight, (((1,), (1,)), ((), ())), preferred_element_type=jnp.float32)
    input_grad = input_sum.astype(jnp.bfloat16)
    gram = lax.dot_general(cotangent, cotangent, (((0,), (0,)), ((), ())), preferred_element_type=jnp.float32)
    factor = (gram / TOKENS).astype(jnp.bfloat16)
    return input_grad, gate_grad, up_grad, down_grad, factor
```

```python
import functools

import jax
import jax.numpy as jnp
from jax import lax
from jax.experimental import pallas as pl
from jax.experimental.pallas import tpu as pltpu
from jax.sharding import PartitionSpec as P

MESH = pl.DeviceIdType.MESH
FOLD = 8
F32 = jnp.float32
BF16 = jnp.bfloat16


def exchange_kernel(
    n,
    cot_ref, inp_ref, gate_ref, up_ref, gw_hbm, uw_hbm, dw_hbm,
    cot_out, inp_out, hidden_out, gd_out, ud_out, owned_out, ig_out,
    cot_g, inp_g, gw, uw, dw, acc, stack, part, landed,
    w_sem, cot_send, cot_recv, inp_send, inp_recv, rs_send, rs_recv,
):
    me = lax.axis_index("tensor")
    blk, width = cot_ref.shape
    tokens = cot_out.shape[0]

    dw_copy = pltpu.make_async_copy(dw_hbm, dw, w_sem.at[0])
    gw_copy = pltpu.make_async_copy(gw_hbm, gw, w_sem.at[1])
    uw_copy = pltpu.make_async_copy(uw_hbm, uw, w_sem.at[2])
    dw_copy.start()
    gw_copy.start()
    uw_copy.start()

    def peer(k):
        return lax.rem(me + k, n)

    def rows(p):
        return pl.ds(pl.multiple_of(p * blk, blk), blk)

    barrier = pltpu.get_barrier_semaphore()

    @pl.loop(1, n)
    def _(k):
        pl.semaphore_signal(barrier, inc=1, device_id={"tensor": peer(k)}, device_id_type=MESH)

    pl.semaphore_wait(barrier, n - 1)

    def send(src, dst, send_sem, recv_sem, k):
        return pltpu.make_async_remote_copy(
            src_ref=src, dst_ref=dst.at[rows(me)],
            send_sem=send_sem.at[k], recv_sem=recv_sem.at[me],
            device_id={"tensor": peer(k)}, device_id_type=MESH,
        )

    def arrival(dst, send_sem, recv_sem, k):
        p = peer(k)
        return pltpu.make_async_remote_copy(
            src_ref=dst.at[rows(p)], dst_ref=dst.at[rows(p)],
            send_sem=send_sem.at[k], recv_sem=recv_sem.at[p],
            device_id={"tensor": p}, device_id_type=MESH,
        )

    @pl.loop(1, n)
    def _(k):
        send(cot_ref, cot_g, cot_send, cot_recv, k).start()

    @pl.loop(1, n)
    def _(k):
        send(inp_ref, inp_g, inp_send, inp_recv, k).start()

    cot_g[rows(me), :] = cot_ref[...]
    inp_g[rows(me), :] = inp_ref[...]

    size = tokens * FOLD
    first = lax.broadcasted_iota(jnp.int32, (size, size), 0)
    second = lax.broadcasted_iota(jnp.int32, (size, size), 1)

    def unfold(src, dst):
        pick = (second == (first % tokens) * FOLD + first // tokens).astype(BF16)
        wide = jnp.dot(pick, src[...], preferred_element_type=F32).astype(BF16)
        for c in range(FOLD):
            dst[:, c * width:(c + 1) * width] = wide[c * tokens:(c + 1) * tokens]

    gate = gate_ref[...].astype(F32)
    up = up_ref[...].astype(F32)
    sigma = 1.0 / (1.0 + jnp.exp(-gate))
    act = gate * sigma
    hidden_out[...] = (act * up).astype(BF16)

    @pl.loop(1, n)
    def _(k):
        arrival(cot_g, cot_send, cot_recv, k).wait_recv()

    unfold(cot_g, cot_out)
    if owned_out is not None:
        own = owned_out.shape[1]
        owned_out[...] = cot_out[:, pl.ds(pl.multiple_of(me * own, own), own)]

    dw_copy.wait()
    acc[...] = jnp.zeros_like(acc)

    @pl.loop(0, FOLD)
    def _(c):
        cols = pl.ds(pl.multiple_of(c * width, width), width)
        acc[...] += lax.dot_general(
            cot_out[:, cols], dw[:, cols], (((1,), (1,)), ((), ())), preferred_element_type=F32
        )

    hg = acc[...]
    gd_out[...] = (hg * up * sigma * (1.0 + gate * (1.0 - sigma))).astype(BF16)
    ud_out[...] = (hg * act).astype(BF16)

    gw_copy.wait()
    uw_copy.wait()

    @pl.loop(0, FOLD)
    def _(c):
        here = pl.ds(pl.multiple_of(c * width, width), width)
        total = lax.dot_general(
            gd_out[...], gw[here, :], (((1,), (1,)), ((), ())), preferred_element_type=F32
        ) + lax.dot_general(
            ud_out[...], uw[here, :], (((1,), (1,)), ((), ())), preferred_element_type=F32
        )
        stack[pl.ds(pl.multiple_of(c * tokens, tokens), tokens), :] = total.astype(BF16)

    back = (second == (first % FOLD) * tokens + first // FOLD).astype(BF16)
    part[...] = jnp.dot(back, stack[...], preferred_element_type=F32).astype(BF16)

    def reduce_send(k):
        return pltpu.make_async_remote_copy(
            src_ref=part.at[rows(peer(k))], dst_ref=landed.at[rows(me)],
            send_sem=rs_send.at[k], recv_sem=rs_recv.at[me],
            device_id={"tensor": peer(k)}, device_id_type=MESH,
        )

    @pl.loop(1, n)
    def _(k):
        reduce_send(k).start()

    @pl.loop(1, n)
    def _(k):
        arrival(inp_g, inp_send, inp_recv, k).wait_recv()

    unfold(inp_g, inp_out)

    landed[rows(me), :] = part[rows(me), :]

    @pl.loop(1, n)
    def _(k):
        arrival(landed, rs_send, rs_recv, k).wait_recv()

    def add(p, total):
        return total + landed[rows(p), :].astype(F32)

    ig_out[...] = lax.fori_loop(0, n, add, jnp.zeros((blk, width), F32)).astype(BF16)

    @pl.loop(1, n)
    def _(k):
        send(cot_ref, cot_g, cot_send, cot_recv, k).wait_send()
        send(inp_ref, inp_g, inp_send, inp_recv, k).wait_send()
        reduce_send(k).wait_send()


def grads_kernel(tokens, cot_ref, inp_ref, hidden_ref, gd_ref, ud_ref, owned_ref,
                 gg_out, ug_out, dg_out, fac_out):
    dims = (((0,), (0,)), ((), ()))
    x = inp_ref[...]
    y = cot_ref[...]
    gg_out[...] = lax.dot_general(x, gd_ref[...], dims, preferred_element_type=F32).astype(BF16)
    ug_out[...] = lax.dot_general(x, ud_ref[...], dims, preferred_element_type=F32).astype(BF16)
    dg_out[...] = lax.dot_general(hidden_ref[...], y, dims, preferred_element_type=F32).astype(BF16)
    gram = lax.dot_general(owned_ref[...], y, dims, preferred_element_type=F32)
    if tokens & (tokens - 1) == 0:
        gram = gram * (1.0 / tokens)
    else:
        gram = gram / tokens
    fac_out[...] = gram.astype(BF16)


def per_device(n, layer_input, cotangent, gate_values, up_values, gate_weight, up_weight, down_weight):
    local, d = cotangent.shape
    tokens, ff = gate_values.shape
    width = d // FOLD
    blk = local * FOLD
    own = d // n
    inside = own % 128 == 0
    vmem = pl.BlockSpec(memory_space=pltpu.VMEM)
    hbm = pl.BlockSpec(memory_space=pl.ANY)
    shape = jax.ShapeDtypeStruct
    outs = [
        shape((tokens, d), BF16), shape((tokens, d), BF16),
        shape((tokens, ff), BF16), shape((tokens, ff), BF16), shape((tokens, ff), BF16),
        shape((tokens, own), BF16), shape((blk, width), BF16),
    ]
    body = functools.partial(exchange_kernel, n)
    if not inside:
        del outs[5]

        def body(*refs):
            return exchange_kernel(n, *refs[:12], None, *refs[12:])

    gathered = pltpu.VMEM((tokens * FOLD, width), BF16)
    results = pl.pallas_call(
        body,
        out_shape=outs,
        in_specs=[vmem] * 4 + [hbm] * 3,
        out_specs=[vmem] * len(outs),
        scratch_shapes=[
            gathered, gathered,
            pltpu.VMEM((d, ff), BF16), pltpu.VMEM((d, ff), BF16), pltpu.VMEM((ff, d), BF16),
            pltpu.VMEM((tokens, ff), F32),
            gathered, gathered, gathered,
            pltpu.SemaphoreType.DMA((3,)),
        ] + [pltpu.SemaphoreType.DMA((n,))] * 6,
        compiler_params=pltpu.CompilerParams(
            collective_id=0, has_side_effects=True, vmem_limit_bytes=60 * 2**20
        ),
        cost_estimate=pl.CostEstimate(
            flops=6 * tokens * d * ff, bytes_accessed=6 * d * ff, transcendentals=tokens * ff
        ),
        name="exchange",
    )(
        cotangent.reshape(blk, width), layer_input.reshape(blk, width),
        gate_values, up_values, gate_weight, up_weight, down_weight,
    )
    cot, inp, hidden, gd, ud = results[:5]
    if inside:
        owned = results[5]
    else:
        owned = lax.dynamic_slice_in_dim(cot, lax.axis_index("tensor") * own, own, 1)
    input_grad = results[-1].reshape(local, d)

    tile = d // 16
    whole = lambda a: pl.BlockSpec(a.shape, lambda i: (0, 0))
    gate_grad, up_grad, down_grad, factor = pl.pallas_call(
        functools.partial(grads_kernel, tokens),
        grid=(d // tile,),
        out_shape=[
            shape((d, ff), BF16), shape((d, ff), BF16), shape((ff, d), BF16), shape((own, d), BF16),
        ],
        in_specs=[
            pl.BlockSpec((tokens, tile), lambda i: (0, i)),
            pl.BlockSpec((tokens, tile), lambda i: (0, i)),
            whole(hidden), whole(gd), whole(ud), whole(owned),
        ],
        out_specs=[
            pl.BlockSpec((tile, ff), lambda i: (i, 0)),
            pl.BlockSpec((tile, ff), lambda i: (i, 0)),
            pl.BlockSpec((ff, tile), lambda i: (0, i)),
            pl.BlockSpec((own, tile), lambda i: (0, i)),
        ],
        compiler_params=pltpu.CompilerParams(vmem_limit_bytes=48 * 2**20),
        cost_estimate=pl.CostEstimate(
            flops=6 * tokens * d * ff + 2 * tokens * d * own,
            bytes_accessed=6 * d * ff + 2 * d * own, transcendentals=0,
        ),
        name="grads",
    )(cot, inp, hidden, gd, ud, owned)
    return (input_grad, gate_grad, up_grad, down_grad, factor)


def solution(mesh):
    return jax.shard_map(
        functools.partial(per_device, mesh.shape["tensor"]),
        mesh=mesh,
        in_specs=(
            P(("groups", "tensor"), None),
            P(("groups", "tensor"), None),
            P("groups", "tensor"),
            P("groups", "tensor"),
            P("groups", "tensor"),
            P("groups", "tensor"),
            P(("groups", "tensor"), None),
        ),
        out_specs=(
            P(("groups", "tensor"), None),
            P("groups", "tensor"),
            P("groups", "tensor"),
            P(("groups", "tensor"), None),
            P(("groups", "tensor"), None),
        ),
        check_vma=False,
    )
```

```python
import functools

import jax
import jax.numpy as jnp
from jax import lax
from jax.experimental import pallas as pl
from jax.experimental.pallas import tpu as pltpu
from jax.sharding import PartitionSpec as P

MESH = pl.DeviceIdType.MESH
FOLD = 8
PIECES = 4
F32 = jnp.float32
BF16 = jnp.bfloat16


def exchange_kernel(
    n,
    cot_ref, inp_ref, gate_ref, up_ref, gw_hbm, uw_hbm, dw_hbm,
    cot_out, inp_out, hidden_out, gd_out, ud_out, owned_out, ig_out,
    cot_g, inp_g, gw, uw, dw, acc, fold, stack, part, pair, half, landed,
    w_sem, cot_send, cot_recv, inp_send, inp_recv, swap_send, swap_recv,
    pair_send, pair_recv, rs_send, rs_recv,
):
    me = lax.axis_index("tensor")
    local, d = cot_ref.shape
    tokens = cot_out.shape[0]
    width = d // FOLD
    blk = local * FOLD
    chips = n // 2
    side = chips * blk
    step = width // PIECES
    core = lax.rem(me, 2)
    chip = lax.div(me, 2)
    twin = me + 1 - 2 * core

    dw_copy = pltpu.make_async_copy(dw_hbm, dw, w_sem.at[0])
    gw_copy = pltpu.make_async_copy(gw_hbm, gw, w_sem.at[1])
    uw_copy = pltpu.make_async_copy(uw_hbm, uw, w_sem.at[2])
    dw_copy.start()
    gw_copy.start()
    uw_copy.start()

    def there(k):
        return lax.rem(chip + k, chips)

    def device(c):
        return {"tensor": 2 * c + core}

    barrier = pltpu.get_barrier_semaphore()

    @pl.loop(1, chips)
    def _(k):
        pl.semaphore_signal(barrier, inc=1, device_id=device(there(k)), device_id_type=MESH)

    pl.semaphore_signal(barrier, inc=1, device_id={"tensor": twin}, device_id_type=MESH)

    def slot(c):
        return pl.ds(pl.multiple_of(core * side + c * blk, blk), blk)

    def block(c):
        return pl.ds(pl.multiple_of(c * blk, blk), blk)

    mine = pl.ds(pl.multiple_of(core * side, side), side)
    others = pl.ds(pl.multiple_of((1 - core) * side, side), side)

    def place(src, dst):
        x = src[...].astype(F32)
        for c in range(FOLD):
            fold[c * local:(c + 1) * local, :] = x[:, c * width:(c + 1) * width]
        dst[slot(chip), :] = fold[...].astype(BF16)

    def send(buf, send_sem, recv_sem, k):
        return pltpu.make_async_remote_copy(
            src_ref=buf.at[slot(chip)], dst_ref=buf.at[slot(chip)],
            send_sem=send_sem.at[k], recv_sem=recv_sem.at[chip],
            device_id=device(there(k)), device_id_type=MESH,
        )

    def arrival(buf, send_sem, recv_sem, k):
        c = there(k)
        return pltpu.make_async_remote_copy(
            src_ref=buf.at[slot(c)], dst_ref=buf.at[slot(c)],
            send_sem=send_sem.at[k], recv_sem=recv_sem.at[c],
            device_id=device(c), device_id_type=MESH,
        )

    def swap(buf, i, rows):
        return pltpu.make_async_remote_copy(
            src_ref=buf.at[rows], dst_ref=buf.at[rows],
            send_sem=swap_send.at[i], recv_sem=swap_recv.at[i],
            device_id={"tensor": twin}, device_id_type=MESH,
        )

    place(cot_ref, cot_g)
    place(inp_ref, inp_g)
    pl.semaphore_wait(barrier, chips)

    @pl.loop(1, chips)
    def _(k):
        send(cot_g, cot_send, cot_recv, k).start()

    size = tokens * FOLD
    first = lax.broadcasted_iota(jnp.int32, (size, size), 0)
    second = lax.broadcasted_iota(jnp.int32, (size, size), 1)

    def gathered_row(stacked):
        c, t = stacked // tokens, stacked % tokens
        owner, r = t // local, t % local
        return (owner % 2) * side + (owner // 2) * blk + c * local + r

    def unfold(src, dst):
        pick = (second == gathered_row(first)).astype(BF16)
        wide = jnp.dot(pick, src[...], preferred_element_type=F32).astype(BF16)
        for c in range(FOLD):
            dst[:, c * width:(c + 1) * width] = wide[c * tokens:(c + 1) * tokens]

    gate = gate_ref[...].astype(F32)
    up = up_ref[...].astype(F32)
    sigma = 1.0 / (1.0 + jnp.exp(-gate))
    act = gate * sigma
    hidden_out[...] = (act * up).astype(BF16)

    @pl.loop(1, chips)
    def _(k):
        arrival(cot_g, cot_send, cot_recv, k).wait_recv()

    swap(cot_g, 0, mine).start()

    @pl.loop(1, chips)
    def _(k):
        send(inp_g, inp_send, inp_recv, k).start()

    swap(cot_g, 0, others).wait_recv()
    unfold(cot_g, cot_out)
    if owned_out is not None:
        own = owned_out.shape[1]
        owned_out[...] = cot_out[:, pl.ds(pl.multiple_of(me * own, own), own)]

    dw_copy.wait()
    acc[...] = jnp.zeros_like(acc)

    @pl.loop(0, FOLD)
    def _(c):
        cols = pl.ds(pl.multiple_of(c * width, width), width)
        acc[...] += lax.dot_general(
            cot_out[:, cols], dw[:, cols], (((1,), (1,)), ((), ())), preferred_element_type=F32
        )

    hg = acc[...]
    gd_out[...] = (hg * up * sigma * (1.0 + gate * (1.0 - sigma))).astype(BF16)
    ud_out[...] = (hg * act).astype(BF16)

    @pl.loop(1, chips)
    def _(k):
        arrival(inp_g, inp_send, inp_recv, k).wait_recv()

    swap(inp_g, 1, mine).start()
    gw_copy.wait()
    uw_copy.wait()
    back = (first == gathered_row(second)).astype(BF16)

    def pair_copy(h):
        return pltpu.make_async_remote_copy(
            src_ref=part.at[h, others], dst_ref=pair.at[h],
            send_sem=pair_send.at[h], recv_sem=pair_recv.at[h],
            device_id={"tensor": twin}, device_id_type=MESH,
        )

    def reduce_send(h, k):
        c = there(k)
        return pltpu.make_async_remote_copy(
            src_ref=half.at[h, block(c)], dst_ref=landed.at[h, block(chip)],
            send_sem=rs_send.at[h, k], recv_sem=rs_recv.at[h, chip],
            device_id=device(c), device_id_type=MESH,
        )

    def reduce_arrival(h, k):
        c = there(k)
        return pltpu.make_async_remote_copy(
            src_ref=landed.at[h, block(c)], dst_ref=landed.at[h, block(c)],
            send_sem=rs_send.at[h, k], recv_sem=rs_recv.at[h, c],
            device_id=device(c), device_id_type=MESH,
        )

    def pass_on(h):
        pair_copy(h).wait_recv()
        both = part[h, mine, :].astype(F32) + pair[h].astype(F32)
        half[h] = both.astype(BF16)

        @pl.loop(1, chips)
        def _(k):
            reduce_send(h, k).start()

    for h in range(PIECES):
        @pl.loop(0, FOLD)
        def _(c):
            here = pl.ds(pl.multiple_of(c * width + h * step, step), step)
            total = lax.dot_general(
                gd_out[...], gw[here, :], (((1,), (1,)), ((), ())), preferred_element_type=F32
            ) + lax.dot_general(
                ud_out[...], uw[here, :], (((1,), (1,)), ((), ())), preferred_element_type=F32
            )
            stack[pl.ds(pl.multiple_of(c * tokens, tokens), tokens), :] = total.astype(BF16)

        part[h] = jnp.dot(back, stack[...], preferred_element_type=F32).astype(BF16)
        pair_copy(h).start()
        if h:
            pass_on(h - 1)

    pass_on(PIECES - 1)
    swap(inp_g, 1, others).wait_recv()
    unfold(inp_g, inp_out)

    for h in range(PIECES):
        @pl.loop(1, chips)
        def _(k):
            reduce_arrival(h, k).wait_recv()

        def add(k, total):
            return total + landed[h, block(there(k)), :].astype(F32)

        total = lax.fori_loop(1, chips, add, half[h, block(chip), :].astype(F32))
        fold[:, h * step:(h + 1) * step] = total

    for c in range(FOLD):
        ig_out[:, c * width:(c + 1) * width] = fold[c * local:(c + 1) * local, :].astype(BF16)

    @pl.loop(1, chips)
    def _(k):
        send(cot_g, cot_send, cot_recv, k).wait_send()
        send(inp_g, inp_send, inp_recv, k).wait_send()
        for h in range(PIECES):
            reduce_send(h, k).wait_send()

    swap(cot_g, 0, mine).wait_send()
    swap(inp_g, 1, mine).wait_send()
    for h in range(PIECES):
        pair_copy(h).wait_send()


def grads_kernel(tokens, cot_ref, inp_ref, hidden_ref, gd_ref, ud_ref, owned_ref,
                 gg_out, ug_out, dg_out, fac_out):
    dims = (((0,), (0,)), ((), ()))
    x = inp_ref[...]
    y = cot_ref[...]
    gg_out[...] = lax.dot_general(x, gd_ref[...], dims, preferred_element_type=F32).astype(BF16)
    ug_out[...] = lax.dot_general(x, ud_ref[...], dims, preferred_element_type=F32).astype(BF16)
    dg_out[...] = lax.dot_general(hidden_ref[...], y, dims, preferred_element_type=F32).astype(BF16)
    gram = lax.dot_general(owned_ref[...], y, dims, preferred_element_type=F32)
    if tokens & (tokens - 1) == 0:
        gram = gram * (1.0 / tokens)
    else:
        gram = gram / tokens
    fac_out[...] = gram.astype(BF16)


def per_device(n, layer_input, cotangent, gate_values, up_values, gate_weight, up_weight, down_weight):
    local, d = cotangent.shape
    tokens, ff = gate_values.shape
    width = d // FOLD
    blk = local * FOLD
    step = width // PIECES
    own = d // n
    inside = own % 128 == 0
    vmem = pl.BlockSpec(memory_space=pltpu.VMEM)
    hbm = pl.BlockSpec(memory_space=pl.ANY)
    shape = jax.ShapeDtypeStruct
    outs = [
        shape((tokens, d), BF16), shape((tokens, d), BF16),
        shape((tokens, ff), BF16), shape((tokens, ff), BF16), shape((tokens, ff), BF16),
        shape((tokens, own), BF16), shape((local, d), BF16),
    ]
    body = functools.partial(exchange_kernel, n)
    if not inside:
        del outs[5]

        def body(*refs):
            return exchange_kernel(n, *refs[:12], None, *refs[12:])

    gathered = pltpu.VMEM((tokens * FOLD, width), BF16)
    results = pl.pallas_call(
        body,
        out_shape=outs,
        in_specs=[vmem] * 4 + [hbm] * 3,
        out_specs=[vmem] * len(outs),
        scratch_shapes=[
            gathered, gathered,
            pltpu.VMEM((d, ff), BF16), pltpu.VMEM((d, ff), BF16), pltpu.VMEM((ff, d), BF16),
            pltpu.VMEM((tokens, ff), F32),
            pltpu.VMEM((blk, width), F32),
            pltpu.VMEM((tokens * FOLD, step), BF16),
            pltpu.VMEM((PIECES, tokens * FOLD, step), BF16),
        ] + [pltpu.VMEM((PIECES, tokens * FOLD // 2, step), BF16)] * 3
        + [pltpu.SemaphoreType.DMA((3,))]
        + [pltpu.SemaphoreType.DMA((n // 2,))] * 4
        + [pltpu.SemaphoreType.DMA((2,))] * 2
        + [pltpu.SemaphoreType.DMA((PIECES,))] * 2
        + [pltpu.SemaphoreType.DMA((PIECES, n // 2))] * 2,
        compiler_params=pltpu.CompilerParams(
            collective_id=0, has_side_effects=True, vmem_limit_bytes=60 * 2**20
        ),
        cost_estimate=pl.CostEstimate(
            flops=6 * tokens * d * ff, bytes_accessed=6 * d * ff, transcendentals=tokens * ff
        ),
        name="exchange",
    )(
        cotangent, layer_input, gate_values, up_values, gate_weight, up_weight, down_weight,
    )
    cot, inp, hidden, gd, ud = results[:5]
    if inside:
        owned = results[5]
    else:
        owned = lax.dynamic_slice_in_dim(cot, lax.axis_index("tensor") * own, own, 1)
    input_grad = results[-1]

    tile = d // 16
    whole = lambda a: pl.BlockSpec(a.shape, lambda i: (0, 0))
    gate_grad, up_grad, down_grad, factor = pl.pallas_call(
        functools.partial(grads_kernel, tokens),
        grid=(d // tile,),
        out_shape=[
            shape((d, ff), BF16), shape((d, ff), BF16), shape((ff, d), BF16), shape((own, d), BF16),
        ],
        in_specs=[
            pl.BlockSpec((tokens, tile), lambda i: (0, i)),
            pl.BlockSpec((tokens, tile), lambda i: (0, i)),
            whole(hidden), whole(gd), whole(ud), whole(owned),
        ],
        out_specs=[
            pl.BlockSpec((tile, ff), lambda i: (i, 0)),
            pl.BlockSpec((tile, ff), lambda i: (i, 0)),
            pl.BlockSpec((ff, tile), lambda i: (0, i)),
            pl.BlockSpec((own, tile), lambda i: (0, i)),
        ],
        compiler_params=pltpu.CompilerParams(vmem_limit_bytes=60 * 2**20),
        cost_estimate=pl.CostEstimate(
            flops=6 * tokens * d * ff + 2 * tokens * d * own,
            bytes_accessed=6 * d * ff + 2 * d * own, transcendentals=0,
        ),
        name="grads",
    )(cot, inp, hidden, gd, ud, owned)
    return (input_grad, gate_grad, up_grad, down_grad, factor)


def solution(mesh):
    return jax.shard_map(
        functools.partial(per_device, mesh.shape["tensor"]),
        mesh=mesh,
        in_specs=(
            P(("groups", "tensor"), None),
            P(("groups", "tensor"), None),
            P("groups", "tensor"),
            P("groups", "tensor"),
            P("groups", "tensor"),
            P("groups", "tensor"),
            P(("groups", "tensor"), None),
        ),
        out_specs=(
            P(("groups", "tensor"), None),
            P("groups", "tensor"),
            P("groups", "tensor"),
            P(("groups", "tensor"), None),
            P(("groups", "tensor"), None),
        ),
        check_vma=False,
    )
```

```python
import functools

import jax
import jax.numpy as jnp
from jax import lax
from jax.experimental import pallas as pl
from jax.experimental.pallas import tpu as pltpu
from jax.sharding import PartitionSpec as P

MESH = pl.DeviceIdType.MESH
FOLD = 8
PIECES = 4
F32 = jnp.float32
BF16 = jnp.bfloat16


def exchange_kernel(
    n,
    cot_ref, inp_ref, gate_ref, up_ref, gw_hbm, uw_hbm, dw_hbm,
    cot_out, inp_out, hidden_out, gd_out, ud_out, owned_out, ig_out,
    cot_g, inp_g, gw, uw, dw, acc, fold, stack, part, pair, half, landed,
    w_sem, cot_send, cot_recv, inp_send, inp_recv, swap_send, swap_recv,
    pair_send, pair_recv, rs_send, rs_recv,
):
    me = lax.axis_index("tensor")
    local, d = cot_ref.shape
    tokens = cot_out.shape[0]
    width = d // FOLD
    blk = local * FOLD
    chips = n // 2
    side = chips * blk
    step = width // PIECES
    core = lax.rem(me, 2)
    chip = lax.div(me, 2)
    twin = me + 1 - 2 * core

    dw_copy = pltpu.make_async_copy(dw_hbm, dw, w_sem.at[0])
    gw_copy = pltpu.make_async_copy(gw_hbm, gw, w_sem.at[1])
    uw_copy = pltpu.make_async_copy(uw_hbm, uw, w_sem.at[2])
    dw_copy.start()
    gw_copy.start()
    uw_copy.start()

    def there(k):
        return lax.rem(chip + k, chips)

    def device(c):
        return {"tensor": 2 * c + core}

    barrier = pltpu.get_barrier_semaphore()

    @pl.loop(1, chips)
    def _(k):
        pl.semaphore_signal(barrier, inc=1, device_id=device(there(k)), device_id_type=MESH)

    pl.semaphore_signal(barrier, inc=1, device_id={"tensor": twin}, device_id_type=MESH)

    def slot(c):
        return pl.ds(pl.multiple_of(core * side + c * blk, blk), blk)

    def block(c):
        return pl.ds(pl.multiple_of(c * blk, blk), blk)

    mine = pl.ds(pl.multiple_of(core * side, side), side)
    others = pl.ds(pl.multiple_of((1 - core) * side, side), side)

    def place(src, dst):
        x = src[...].astype(F32)
        for c in range(FOLD):
            fold[c * local:(c + 1) * local, :] = x[:, c * width:(c + 1) * width]
        dst[slot(chip), :] = fold[...].astype(BF16)

    def send(buf, send_sem, recv_sem, k):
        return pltpu.make_async_remote_copy(
            src_ref=buf.at[slot(chip)], dst_ref=buf.at[slot(chip)],
            send_sem=send_sem.at[k], recv_sem=recv_sem.at[chip],
            device_id=device(there(k)), device_id_type=MESH,
        )

    def arrival(buf, send_sem, recv_sem, k):
        c = there(k)
        return pltpu.make_async_remote_copy(
            src_ref=buf.at[slot(c)], dst_ref=buf.at[slot(c)],
            send_sem=send_sem.at[k], recv_sem=recv_sem.at[c],
            device_id=device(c), device_id_type=MESH,
        )

    def swap(buf, i, rows):
        return pltpu.make_async_remote_copy(
            src_ref=buf.at[rows], dst_ref=buf.at[rows],
            send_sem=swap_send.at[i], recv_sem=swap_recv.at[i],
            device_id={"tensor": twin}, device_id_type=MESH,
        )

    place(cot_ref, cot_g)
    place(inp_ref, inp_g)
    pl.semaphore_wait(barrier, chips)

    @pl.loop(1, chips)
    def _(k):
        send(cot_g, cot_send, cot_recv, k).start()

    size = tokens * FOLD
    first = lax.broadcasted_iota(jnp.int32, (size, size), 0)
    second = lax.broadcasted_iota(jnp.int32, (size, size), 1)

    def gathered_row(stacked):
        c, t = stacked // tokens, stacked % tokens
        owner, r = t // local, t % local
        return (owner % 2) * side + (owner // 2) * blk + c * local + r

    def unfold(src, dst):
        pick = (second == gathered_row(first)).astype(BF16)
        wide = jnp.dot(pick, src[...], preferred_element_type=F32).astype(BF16)
        for c in range(FOLD):
            dst[:, c * width:(c + 1) * width] = wide[c * tokens:(c + 1) * tokens]

    gate = gate_ref[...].astype(F32)
    up = up_ref[...].astype(F32)
    sigma = 1.0 / (1.0 + jnp.exp(-gate))
    act = gate * sigma
    hidden_out[...] = (act * up).astype(BF16)

    @pl.loop(1, chips)
    def _(k):
        arrival(cot_g, cot_send, cot_recv, k).wait_recv()

    swap(cot_g, 0, mine).start()

    @pl.loop(1, chips)
    def _(k):
        send(inp_g, inp_send, inp_recv, k).start()

    swap(cot_g, 0, others).wait_recv()
    unfold(cot_g, cot_out)
    if owned_out is not None:
        own = owned_out.shape[1]
        owned_out[...] = cot_out[:, pl.ds(pl.multiple_of(me * own, own), own)]

    dw_copy.wait()
    acc[...] = jnp.zeros_like(acc)

    @pl.loop(0, FOLD)
    def _(c):
        cols = pl.ds(pl.multiple_of(c * width, width), width)
        acc[...] += lax.dot_general(
            cot_out[:, cols], dw[:, cols], (((1,), (1,)), ((), ())), preferred_element_type=F32
        )

    hg = acc[...]
    gd_out[...] = (hg * up * sigma * (1.0 + gate * (1.0 - sigma))).astype(BF16)
    ud_out[...] = (hg * act).astype(BF16)

    gw_copy.wait()
    uw_copy.wait()
    back = (first == gathered_row(second)).astype(BF16)

    def pair_copy(h):
        return pltpu.make_async_remote_copy(
            src_ref=part.at[h, others], dst_ref=pair.at[h],
            send_sem=pair_send.at[h], recv_sem=pair_recv.at[h],
            device_id={"tensor": twin}, device_id_type=MESH,
        )

    def reduce_send(h, k):
        c = there(k)
        return pltpu.make_async_remote_copy(
            src_ref=half.at[h, block(c)], dst_ref=landed.at[h, block(chip)],
            send_sem=rs_send.at[h, k], recv_sem=rs_recv.at[h, chip],
            device_id=device(c), device_id_type=MESH,
        )

    def reduce_arrival(h, k):
        c = there(k)
        return pltpu.make_async_remote_copy(
            src_ref=landed.at[h, block(c)], dst_ref=landed.at[h, block(c)],
            send_sem=rs_send.at[h, k], recv_sem=rs_recv.at[h, c],
            device_id=device(c), device_id_type=MESH,
        )

    def pass_on(h):
        pair_copy(h).wait_recv()
        both = part[h, mine, :].astype(F32) + pair[h].astype(F32)
        half[h] = both.astype(BF16)

        @pl.loop(1, chips)
        def _(k):
            reduce_send(h, k).start()

    for h in range(PIECES):
        @pl.loop(0, FOLD)
        def _(c):
            here = pl.ds(pl.multiple_of(c * width + h * step, step), step)
            total = lax.dot_general(
                gd_out[...], gw[here, :], (((1,), (1,)), ((), ())), preferred_element_type=F32
            ) + lax.dot_general(
                ud_out[...], uw[here, :], (((1,), (1,)), ((), ())), preferred_element_type=F32
            )
            stack[pl.ds(pl.multiple_of(c * tokens, tokens), tokens), :] = total.astype(BF16)

        part[h] = jnp.dot(back, stack[...], preferred_element_type=F32).astype(BF16)
        pair_copy(h).start()
        if h:
            pass_on(h - 1)

    pass_on(PIECES - 1)

    @pl.loop(1, chips)
    def _(k):
        arrival(inp_g, inp_send, inp_recv, k).wait_recv()

    swap(inp_g, 1, mine).start()
    swap(inp_g, 1, others).wait_recv()
    unfold(inp_g, inp_out)

    for h in range(PIECES):
        @pl.loop(1, chips)
        def _(k):
            reduce_arrival(h, k).wait_recv()

        def add(k, total):
            return total + landed[h, block(there(k)), :].astype(F32)

        total = lax.fori_loop(1, chips, add, half[h, block(chip), :].astype(F32))
        fold[:, h * step:(h + 1) * step] = total

    for c in range(FOLD):
        ig_out[:, c * width:(c + 1) * width] = fold[c * local:(c + 1) * local, :].astype(BF16)

    @pl.loop(1, chips)
    def _(k):
        send(cot_g, cot_send, cot_recv, k).wait_send()
        send(inp_g, inp_send, inp_recv, k).wait_send()
        for h in range(PIECES):
            reduce_send(h, k).wait_send()

    swap(cot_g, 0, mine).wait_send()
    swap(inp_g, 1, mine).wait_send()
    for h in range(PIECES):
        pair_copy(h).wait_send()


def grads_kernel(tokens, cot_ref, inp_ref, hidden_ref, gd_ref, ud_ref, owned_ref,
                 gg_out, ug_out, dg_out, fac_out):
    dims = (((0,), (0,)), ((), ()))
    x = inp_ref[...]
    y = cot_ref[...]
    gg_out[...] = lax.dot_general(x, gd_ref[...], dims, preferred_element_type=F32).astype(BF16)
    ug_out[...] = lax.dot_general(x, ud_ref[...], dims, preferred_element_type=F32).astype(BF16)
    dg_out[...] = lax.dot_general(hidden_ref[...], y, dims, preferred_element_type=F32).astype(BF16)
    gram = lax.dot_general(owned_ref[...], y, dims, preferred_element_type=F32)
    if tokens & (tokens - 1) == 0:
        gram = gram * (1.0 / tokens)
    else:
        gram = gram / tokens
    fac_out[...] = gram.astype(BF16)


def per_device(n, layer_input, cotangent, gate_values, up_values, gate_weight, up_weight, down_weight):
    local, d = cotangent.shape
    tokens, ff = gate_values.shape
    width = d // FOLD
    blk = local * FOLD
    step = width // PIECES
    own = d // n
    inside = own % 128 == 0
    vmem = pl.BlockSpec(memory_space=pltpu.VMEM)
    hbm = pl.BlockSpec(memory_space=pl.ANY)
    shape = jax.ShapeDtypeStruct
    outs = [
        shape((tokens, d), BF16), shape((tokens, d), BF16),
        shape((tokens, ff), BF16), shape((tokens, ff), BF16), shape((tokens, ff), BF16),
        shape((tokens, own), BF16), shape((local, d), BF16),
    ]
    body = functools.partial(exchange_kernel, n)
    if not inside:
        del outs[5]

        def body(*refs):
            return exchange_kernel(n, *refs[:12], None, *refs[12:])

    gathered = pltpu.VMEM((tokens * FOLD, width), BF16)
    results = pl.pallas_call(
        body,
        out_shape=outs,
        in_specs=[vmem] * 4 + [hbm] * 3,
        out_specs=[vmem] * len(outs),
        scratch_shapes=[
            gathered, gathered,
            pltpu.VMEM((d, ff), BF16), pltpu.VMEM((d, ff), BF16), pltpu.VMEM((ff, d), BF16),
            pltpu.VMEM((tokens, ff), F32),
            pltpu.VMEM((blk, width), F32),
            pltpu.VMEM((tokens * FOLD, step), BF16),
            pltpu.VMEM((PIECES, tokens * FOLD, step), BF16),
        ] + [pltpu.VMEM((PIECES, tokens * FOLD // 2, step), BF16)] * 3
        + [pltpu.SemaphoreType.DMA((3,))]
        + [pltpu.SemaphoreType.DMA((n // 2,))] * 4
        + [pltpu.SemaphoreType.DMA((2,))] * 2
        + [pltpu.SemaphoreType.DMA((PIECES,))] * 2
        + [pltpu.SemaphoreType.DMA((PIECES, n // 2))] * 2,
        compiler_params=pltpu.CompilerParams(
            collective_id=0, has_side_effects=True, vmem_limit_bytes=60 * 2**20
        ),
        cost_estimate=pl.CostEstimate(
            flops=6 * tokens * d * ff, bytes_accessed=6 * d * ff, transcendentals=tokens * ff
        ),
        name="exchange",
    )(
        cotangent, layer_input, gate_values, up_values, gate_weight, up_weight, down_weight,
    )
    cot, inp, hidden, gd, ud = results[:5]
    if inside:
        owned = results[5]
    else:
        owned = lax.dynamic_slice_in_dim(cot, lax.axis_index("tensor") * own, own, 1)
    input_grad = results[-1]

    tile = d // 8
    whole = lambda a: pl.BlockSpec(a.shape, lambda i: (0, 0))
    gate_grad, up_grad, down_grad, factor = pl.pallas_call(
        functools.partial(grads_kernel, tokens),
        grid=(d // tile,),
        out_shape=[
            shape((d, ff), BF16), shape((d, ff), BF16), shape((ff, d), BF16), shape((own, d), BF16),
        ],
        in_specs=[
            pl.BlockSpec((tokens, tile), lambda i: (0, i)),
            pl.BlockSpec((tokens, tile), lambda i: (0, i)),
            whole(hidden), whole(gd), whole(ud), whole(owned),
        ],
        out_specs=[
            pl.BlockSpec((tile, ff), lambda i: (i, 0)),
            pl.BlockSpec((tile, ff), lambda i: (i, 0)),
            pl.BlockSpec((ff, tile), lambda i: (0, i)),
            pl.BlockSpec((own, tile), lambda i: (0, i)),
        ],
        compiler_params=pltpu.CompilerParams(vmem_limit_bytes=60 * 2**20),
        cost_estimate=pl.CostEstimate(
            flops=6 * tokens * d * ff + 2 * tokens * d * own,
            bytes_accessed=6 * d * ff + 2 * d * own, transcendentals=0,
        ),
        name="grads",
    )(cot, inp, hidden, gd, ud, owned)
    return (input_grad, gate_grad, up_grad, down_grad, factor)


def solution(mesh):
    return jax.shard_map(
        functools.partial(per_device, mesh.shape["tensor"]),
        mesh=mesh,
        in_specs=(
            P(("groups", "tensor"), None),
            P(("groups", "tensor"), None),
            P("groups", "tensor"),
            P("groups", "tensor"),
            P("groups", "tensor"),
            P("groups", "tensor"),
            P(("groups", "tensor"), None),
        ),
        out_specs=(
            P(("groups", "tensor"), None),
            P("groups", "tensor"),
            P("groups", "tensor"),
            P(("groups", "tensor"), None),
            P(("groups", "tensor"), None),
        ),
        check_vma=False,
    )
```
